256 devices in a mesh: date: 4 (over x), prod: 64 (over z, y, core).
Axes of the slice: x: 4, y: 4, z: 8, core: 2. Of those that a mesh axis runs over, the one named last changes fastest.
Arguments:
- cash_codes: int32 [524288, 128], P('prod'), may hold values from -127 to 127
- block_scales: float32 [524288, 4], P('prod'), may hold values from 8.286408e-05 to 0.00082864077
- trade_kind: int32 [524288], P('prod'), may hold values 0 or 1
- strike: float32 [524288], P('prod'), may hold values from -0.1875 to 0.1875
- set_of_trade: int32 [524288], P('prod'), may hold values from 0 to 2047
- discount: bfloat16 [16, 128, 64], P('date'), may hold values from 0.29882812 to 1
- lag_dates: int32 [2048], P('prod'), may hold values from 1 to 2, as said below
- threshold: float32 [2048], P('prod'), may hold values from 0.3 to 3
Outputs:
- exposure: float32 [16, 2048, 64], P('date', 'prod')
The draws below stay inside these ranges and needn't reach their ends.
Inputs may be any that keep to these rules, and one draw needn't show every extreme that they name: `lag_dates`: every draw holds some set with a margin period of 2 dates.
All inputs are finite; a program needn't handle non-finite values. No bound on the sum of `trade_kind` on one device may be relied on, other than what follows from the above.
Results may differ from the reference program's by a relative error of at most 0.0023.
Values sent between devices are 32-bit elements; how exact they have to be, the bound alone decides.
A program may use at most 64 MiB of HBM per device.

```python
import math
import jax
import jax.numpy as jnp
from jax import lax

P_SIZE = 64
K = 128
BLOCK = 32
LAGMAX = 2
DATES = 16
TRADES = 524288
SETS = 2048


def draw_lag_dates(key, part):
    key = jax.random.fold_in(key, 7)
    first_key, second_key = jax.random.split(key)
    periods = jax.random.randint(first_key, (SETS,), 1, LAGMAX + 1)
    where_most = jax.random.randint(second_key, (), 0, SETS)
    return periods.at[where_most].set(LAGMAX).astype(jnp.int32)


def plant(result, stream_key, smallest, high):
    longest = result.shape.index(max(result.shape))
    spots = []
    for shift in (0, 1):
        where = [jax.random.randint(jax.random.fold_in(stream_key, axis), (), 0, length) for axis, length in enumerate(result.shape)]
        where[longest] = (where[longest] + shift) % result.shape[longest]
        spots.append(tuple(where))
    return result.at[spots[0]].set(smallest).at[spots[1]].set(high)


def block_levels(own_key, shape, shards, low, high):
    def one(dim, blocks):
        draws = jax.random.uniform(jax.random.fold_in(jax.random.fold_in(own_key, 6), dim), (blocks,), jnp.float32, low / len(shards), high / len(shards))
        return jnp.repeat(jnp.exp(draws), shape[dim] // blocks).reshape((-1,) + (1,) * (len(shape) - dim - 1))

    factor_of = one(*shards[0])
    for cut in shards[1:]:
        factor_of = factor_of * one(*cut)
    return factor_of


def setup_inputs(seed: int = 0) -> dict:
    arg_keys = jax.random.split(jax.random.key(seed), 9)
    return {
        "cash_codes": plant(jax.random.randint(arg_keys[0], (TRADES, K), -127, 128), jax.random.fold_in(arg_keys[0], 1), -127, 127).astype(jnp.int32),
        "block_scales": jnp.clip(jnp.exp(math.log(0.00082864077) - 2.3025851 * jax.random.uniform(arg_keys[1], (TRADES, K // BLOCK), jnp.float32) ** block_levels(arg_keys[1], (TRADES, K // BLOCK), ((0, 64),), -0.2, 0.2)), 8.286407683044672e-05, 0.00082864077),
        "trade_kind": plant((jax.random.randint(arg_keys[2], (TRADES,), 0, 2) < 1).astype(jnp.int32), jax.random.fold_in(arg_keys[2], 1), 0, 1),
        "strike": jnp.clip(jax.random.uniform(arg_keys[3], (TRADES,), jnp.float32, -0.1875, 0.1875) * block_levels(arg_keys[3], (TRADES,), ((0, 64),), -0.4, 0.0), -0.1875, 0.1875),
        "set_of_trade": plant(jax.random.randint(arg_keys[4], (TRADES,), 0, SETS), jax.random.fold_in(arg_keys[4], 1), 0, SETS - 1).astype(jnp.int32),
        "discount": jnp.clip(jnp.exp(math.log(1.0) - 1.2078867 * jax.random.uniform(arg_keys[5], (DATES, K, P_SIZE), jnp.float32) ** block_levels(arg_keys[5], (DATES, K, P_SIZE), ((0, 4),), -0.2, 0.2)), 0.29882812, 1.0).astype(jnp.bfloat16),
        "lag_dates": draw_lag_dates(jax.random.fold_in(arg_keys[8], 71), 0),
        "threshold": jnp.clip(jnp.exp(math.log(3.0) - 2.3025851 * jax.random.uniform(arg_keys[7], (SETS,), jnp.float32) ** block_levels(arg_keys[7], (SETS,), ((0, 64),), -0.2, 0.2)), 0.3, 3.0),
    }


def reference(cash_codes, block_scales, trade_kind, strike, set_of_trade, discount, lag_dates, threshold):
    cashflow = (cash_codes.astype(jnp.float32) * jnp.repeat(block_scales, BLOCK, axis=1)).astype(jnp.bfloat16)
    bucket_step = K // DATES
    buckets = jnp.arange(K, dtype=jnp.int32)
    option = trade_kind == 1

    def one_date(date_index):
        factors = lax.dynamic_index_in_dim(discount, date_index, 0, keepdims=False)
        alive = buckets >= date_index * bucket_step
        live = jnp.where(alive[:, None], factors, jnp.zeros_like(factors))
        raw_value = jnp.dot(cashflow, live, preferred_element_type=jnp.float32)
        trade_value = jnp.where(option[:, None], jnp.maximum(raw_value - strike[:, None], 0.0), raw_value)
        trade_value = trade_value.astype(jnp.bfloat16).astype(jnp.float32)
        return jax.ops.segment_sum(trade_value, set_of_trade, num_segments=SETS)

    set_value = lax.map(one_date, jnp.arange(DATES, dtype=jnp.int32))
    padded = jnp.concatenate([jnp.zeros((LAGMAX, SETS, P_SIZE), jnp.float32), set_value], axis=0)
    lagged = jnp.zeros((DATES, SETS, P_SIZE), jnp.float32)
    for lag_step in range(1, LAGMAX + 1):
        chosen = (lag_dates == lag_step).astype(jnp.float32)[None, :, None]
        lagged = lagged + chosen * padded[LAGMAX - lag_step:LAGMAX - lag_step + DATES]
    limit = threshold[None, :, None]
    collateral = jnp.maximum(lagged - limit, 0.0) - jnp.maximum(-lagged - limit, 0.0)
    return jnp.maximum(set_value - collateral, 0.0)
```

```python
import jax
import jax.numpy as jnp
from jax import lax
from jax.experimental import pallas as pl
from jax.experimental.pallas import tpu as pltpu
from jax.sharding import PartitionSpec as P

MESH = pl.DeviceIdType.MESH
NT = (((1,), (1,)), ((), ()))
Z, Y, CORES = 8, 4, 2
OWN = 32
TILE = Y * CORES * OWN
CHUNK = 1024
F32, BF16 = jnp.float32, jnp.bfloat16


def place(z, y, core):
    return (z * Y + y) * CORES + core


def kernel(
    codes_hbm, scales_ref, kind_ref, strike_ref, set_ref, live_ref, lag_ref, limit_ref, out_ref,
    codes, values, acc, pair_in, y_in, z_out, z_in, lag_out, lag_in,
    codes_sem, pair_s, pair_r, y_s, y_r, z_s, z_r, lag_s, lag_r,
):
    trades, buckets = codes.shape
    dates, owned, paths = out_ref.shape
    columns = dates * paths
    x = lax.axis_index("date")
    me = lax.axis_index("prod")
    core = lax.rem(me, CORES)
    y = lax.rem(me // CORES, Y)
    z = me // (CORES * Y)
    sibling = place(z, y, 1 - core)
    x_next = lax.rem(x + 1, lax.axis_size("date"))

    loads = []
    for j in range(trades // CHUNK):
        rows = pl.ds(j * CHUNK, CHUNK)
        load = pltpu.make_async_copy(codes_hbm.at[rows], codes.at[rows], codes_sem.at[j])
        load.start()
        loads.append(load)

    barrier = pltpu.get_barrier_semaphore()
    peers = [sibling]
    peers += [place(z, lax.rem(y + j, Y), core) for j in range(1, Y)]
    peers += [place(lax.rem(z + j, Z), y, core) for j in range(1, Z)]
    for peer in peers:
        pl.semaphore_signal(barrier, inc=1, device_id={"prod": peer}, device_id_type=MESH)
    x_last = lax.rem(x + lax.axis_size("date") - 1, lax.axis_size("date"))
    pl.semaphore_signal(barrier, inc=1, device_id={"date": x_last}, device_id_type=MESH)

    total_dates = dates * lax.axis_size("date")
    bucket = lax.broadcasted_iota(jnp.int32, (columns, buckets), 1)
    date = x * dates + lax.broadcasted_iota(jnp.int32, (columns, buckets), 0) // paths
    live = jnp.where(
        bucket >= date * (buckets // total_dates), live_ref[...].astype(F32), 0.0
    ).astype(BF16)
    blocks = scales_ref.shape[0]
    for j in range(trades // CHUNK):
        rows = pl.ds(j * CHUNK, CHUNK)
        loads[j].wait()
        code = codes[rows, :].astype(F32).astype(BF16).T.astype(F32)
        scale = scales_ref[:, rows]
        scale = jnp.concatenate(
            [jnp.broadcast_to(scale[b : b + 1], (buckets // blocks, CHUNK)) for b in range(blocks)],
            axis=0,
        )
        raw = jnp.dot(live, (code * scale).astype(BF16), preferred_element_type=F32)
        floored = jnp.maximum(raw - strike_ref[:, rows], 0.0)
        values[:, rows] = jnp.where(kind_ref[:, rows] == 1, floored, raw).astype(BF16)

    r = lax.broadcasted_iota(jnp.int32, (TILE, 128), 0)
    block = r // OWN
    to_core = jnp.where(block < Y, core, 1 - core)
    label = (lax.rem(y + lax.rem(block, Y), Y) * CORES + to_core) * OWN + lax.rem(r, OWN)

    def tile_z(k):
        far = Z // 2 - (k + 1) // 2
        away = jnp.where(lax.rem(k, 2) == 1, far, Z - far)
        return lax.rem(z + away, Z)

    def pair_copy(k):
        return pltpu.make_async_remote_copy(
            src_ref=acc.at[k, pl.ds(TILE // 2, TILE // 2)], dst_ref=pair_in.at[k],
            send_sem=pair_s.at[k], recv_sem=pair_r.at[k],
            device_id={"prod": sibling}, device_id_type=MESH,
        )

    def y_copy(k, j):
        return pltpu.make_async_remote_copy(
            src_ref=acc.at[k, pl.ds(j * OWN, OWN)], dst_ref=y_in.at[k, j - 1],
            send_sem=y_s.at[k, j - 1], recv_sem=y_r.at[k, j - 1],
            device_id={"prod": place(z, lax.rem(y + j, Y), core)}, device_id_type=MESH,
        )

    def z_copy(k):
        return pltpu.make_async_remote_copy(
            src_ref=z_out.at[k], dst_ref=z_in.at[k], send_sem=z_s.at[k], recv_sem=z_r.at[k],
            device_id={"prod": place(tile_z(k), y, core)}, device_id_type=MESH,
        )

    def after_pair(k):
        pair_copy(k).wait_recv()
        acc[k, : TILE // 2] += pair_in[k]
        for j in (2, 1, 3):
            y_copy(k, j).start()

    def y_total(k):
        for j in range(1, Y):
            y_copy(k, j).wait_recv()
        return acc[k, :OWN] + y_in[k, 0] + y_in[k, 1] + y_in[k, 2]

    def after_y(k):
        z_out[k] = y_total(k)
        z_copy(k).start()

    sets16 = set_ref[...].astype(jnp.int16)

    def step(k, carry):
        wanted = (label + tile_z(k) * TILE).astype(jnp.int16)
        wanted = jnp.concatenate([wanted] * (trades // 128), axis=1)
        member = jnp.where(wanted == sets16, BF16(1), BF16(0))
        acc[k] = lax.dot_general(member, values[...], NT, preferred_element_type=F32)

        @pl.when(k == 0)
        def _():
            pl.semaphore_wait(barrier, len(peers) + 1)

        pair_copy(k).start()

        @pl.when(k >= 1)
        def _():
            after_pair(k - 1)

        @pl.when(k >= 4)
        def _():
            after_y(k - 4)

        return carry

    lax.fori_loop(0, Z, step, 0)
    after_pair(Z - 1)
    for k in range(Z - 4, Z - 1):
        after_y(k)
    total = y_total(Z - 1)
    for k in range(Z - 1):
        z_copy(k).wait_recv()
        total = total + z_in[k]

    half = columns // 2
    lag_out[...] = total[:, half:]
    lag_copy = pltpu.make_async_remote_copy(
        src_ref=lag_out, dst_ref=lag_in, send_sem=lag_s.at[0], recv_sem=lag_r.at[0],
        device_id={"date": x_next}, device_id_type=MESH,
    )
    lag_copy.start()
    diagonal = lax.broadcasted_iota(jnp.int32, (owned, owned), 0) == lax.broadcasted_iota(
        jnp.int32, (owned, owned), 1
    )
    lag = jnp.sum(jnp.where(diagonal, lag_ref[...].astype(F32), 0.0), axis=1, keepdims=True)
    limit = jnp.sum(jnp.where(diagonal, limit_ref[...], 0.0), axis=1, keepdims=True)
    lag_copy.wait_recv()
    previous = jnp.where(x > 0, lag_in[...], 0.0)
    lag_one = jnp.concatenate([previous[:, paths:], total[:, : 3 * paths]], axis=1)
    lag_two = jnp.concatenate([previous, total[:, : 2 * paths]], axis=1)
    lagged = jnp.where(lag == 1.0, lag_one, jnp.where(lag == 2.0, lag_two, 0.0))
    collateral = jnp.maximum(lagged - limit, 0.0) - jnp.maximum(-lagged - limit, 0.0)
    exposure = jnp.maximum(total - collateral, 0.0)
    for d in range(dates):
        out_ref[d] = exposure[:, d * paths : (d + 1) * paths]

    for k in range(Z):
        pair_copy(k).wait_send()
        for j in range(1, Y):
            y_copy(k, j).wait_send()
        if k < Z - 1:
            z_copy(k).wait_send()
    lag_copy.wait_send()


def on_device(cash_codes, block_scales, trade_kind, strike, set_of_trade, discount, lag, limit):
    trades, buckets = cash_codes.shape
    dates, _, paths = discount.shape
    columns = dates * paths
    owned = lag.shape[0]
    live = jnp.swapaxes(discount, 1, 2).reshape(columns, buckets)
    vmem = pl.BlockSpec(memory_space=pltpu.VMEM)
    dma = pltpu.SemaphoreType.DMA
    return pl.pallas_call(
        kernel,
        out_shape=jax.ShapeDtypeStruct((dates, owned, paths), F32),
        in_specs=[pl.BlockSpec(memory_space=pl.ANY)] + [vmem] * 7,
        out_specs=vmem,
        scratch_shapes=[
            pltpu.VMEM((trades, buckets), jnp.int32),
            pltpu.VMEM((columns, trades), BF16),
            pltpu.VMEM((Z, TILE, columns), F32),
            pltpu.VMEM((Z, TILE // 2, columns), F32),
            pltpu.VMEM((Z, Y - 1, OWN, columns), F32),
            pltpu.VMEM((Z - 1, OWN, columns), F32),
            pltpu.VMEM((Z - 1, OWN, columns), F32),
            pltpu.VMEM((OWN, columns // 2), F32),
            pltpu.VMEM((OWN, columns // 2), F32),
            dma((trades // CHUNK,)),
            dma((Z,)), dma((Z,)), dma((Z, Y - 1)), dma((Z, Y - 1)),
            dma((Z - 1,)), dma((Z - 1,)), dma((1,)), dma((1,)),
        ],
        compiler_params=pltpu.CompilerParams(
            collective_id=0, has_side_effects=True, vmem_limit_bytes=50 << 20
        ),
        name="exposure",
    )(
        cash_codes, block_scales.T, trade_kind[None], strike[None], set_of_trade[None], live,
        lag[None], limit[None],
    )


def solution(mesh):
    placed = (
        P("prod", None), P("prod", None), P("prod"), P("prod"), P("prod"),
        P("date", None, None), P("prod"), P("prod"),
    )
    return jax.shard_map(
        on_device, mesh=mesh, in_specs=placed, out_specs=P("date", "prod", None), check_vma=False
    )
```

```python
import jax
import jax.numpy as jnp
from jax import lax
from jax.experimental import pallas as pl
from jax.experimental.pallas import tpu as pltpu
from jax.sharding import PartitionSpec as P

MESH = pl.DeviceIdType.MESH
NT = (((1,), (1,)), ((), ()))
Z, Y, CORES = 8, 4, 2
OWN = 32
CELLS = 4
TILE = CELLS * CORES * OWN
WHOLE = 4
CHUNK = 2048
Y_LAG = 5
EARLY = 2
F32, BF16 = jnp.float32, jnp.bfloat16


def place(z, y, core):
    return (z * Y + y) * CORES + core


def kernel(
    codes_hbm, scales_hbm, kind_hbm, strike_hbm, set_hbm, live_hbm, lag_hbm, limit_hbm, out_ref,
    codes, scales_ref, kind_ref, strike_ref, set_ref, live_ref, lag_ref, limit_ref,
    values, acc, pair_in, y_in, z_out, z_in, lag_out, lag_in,
    codes_sem, small_sem, pair_s, pair_r, y_s, y_r, z_s, z_r, lag_s, lag_r,
):
    trades, buckets = codes.shape
    dates, owned, paths = out_ref.shape
    columns = dates * paths
    half = columns // 2
    x = lax.axis_index("date")
    me = lax.axis_index("prod")
    core = lax.rem(me, CORES)
    y = lax.rem(me // CORES, Y)
    z = me // (CORES * Y)
    sibling = place(z, y, 1 - core)
    x_size = lax.axis_size("date")
    x_next = lax.rem(x + 1, x_size)

    small = []
    for i, (src, dst) in enumerate((
        (live_hbm, live_ref), (scales_hbm, scales_ref), (strike_hbm, strike_ref), (kind_hbm, kind_ref),
        (set_hbm, set_ref), (lag_hbm, lag_ref), (limit_hbm, limit_ref),
    )):
        small.append(pltpu.make_async_copy(src, dst, small_sem.at[i]))
    loads = []
    for j in range(trades // CHUNK):
        rows = pl.ds(j * CHUNK, CHUNK)
        loads.append(pltpu.make_async_copy(codes_hbm.at[rows], codes.at[rows], codes_sem.at[j]))
    loads[0].start()
    for load in small:
        load.start()
    for load in loads[1:]:
        load.start()

    barrier = pltpu.get_barrier_semaphore()
    near = [place(z, lax.rem(y + j, Y), core) for j in range(1, Y)]
    near += [place(lax.rem(z + j, Z), y, core) for j in range(1, Z)]
    for peer in [sibling] + near:
        pl.semaphore_signal(barrier, inc=1, device_id={"prod": peer}, device_id_type=MESH)

    @pl.when(x > 0)
    def _():
        pl.semaphore_signal(barrier, inc=1, device_id={"date": x - 1}, device_id_type=MESH)

    for load in small[:4]:
        load.wait()
    total_dates = dates * x_size
    bucket = lax.broadcasted_iota(jnp.int32, (columns, buckets), 1)
    date = x * dates + lax.broadcasted_iota(jnp.int32, (columns, buckets), 0) // paths
    live = jnp.where(
        bucket >= date * (buckets // total_dates), live_ref[...].astype(F32), 0.0
    ).astype(BF16)
    blocks = scales_ref.shape[0]

    def z_of(i):
        plain = jnp.where(i < z, i, i + 1)
        plain = jnp.where((z == 4) & (i >= 4), 11 - i, plain)
        plain = jnp.where((z == 5) & (i >= 5), 12 - i, plain)
        return jnp.where(i == Z - 1, z, plain)

    def cell(k, i):
        n = jnp.maximum((k - WHOLE) * CELLS + i, 0)
        dy = jnp.where(k < WHOLE, i, jnp.where(k == Z - 1, 0, lax.rem(n, Y - 1) + 1))
        which = jnp.where(k < WHOLE, k, WHOLE + jnp.where(k == Z - 1, i, n // (Y - 1)))
        return dy, which

    own_row = lax.broadcasted_iota(jnp.int32, (OWN, 128), 0)

    def set_sums(k, first, count):
        bases = []
        for i in range(CELLS):
            dy, which = cell(k, i)
            bases.append(place(z_of(which), lax.rem(y + dy, Y), 0) * OWN)
        wanted = jnp.concatenate(
            [own_row + (base + to * OWN) for to in (core, 1 - core) for base in bases], axis=0
        ).astype(jnp.int16)
        wanted = jnp.concatenate([wanted] * (count // 128), axis=1)
        rows = pl.ds(first, count)
        sets = set_ref[:, rows].astype(jnp.int16)
        member = jnp.where(wanted == sets, BF16(1), BF16(0))
        return lax.dot_general(member, values[:, rows], NT, preferred_element_type=F32)

    def early_sums(k, j):
        part = set_sums(k, j * CHUNK, CHUNK)
        acc[k] = part if j == 0 else acc[k] + part

    for j in range(trades // CHUNK):
        rows = pl.ds(j * CHUNK, CHUNK)
        loads[j].wait()
        code = codes[rows, :].astype(F32).astype(BF16).T.astype(F32)
        scale = scales_ref[:, rows]
        scale = jnp.concatenate(
            [jnp.broadcast_to(scale[b : b + 1], (buckets // blocks, CHUNK)) for b in range(blocks)],
            axis=0,
        )
        raw = jnp.dot(live, (code * scale).astype(BF16), preferred_element_type=F32)
        floored = jnp.maximum(raw - strike_ref[:, rows], 0.0)
        values[:, rows] = jnp.where(kind_ref[:, rows] == 1, floored, raw).astype(BF16)
        if j == 0:
            for load in small[4:]:
                load.wait()
        else:
            for k in range(EARLY):
                early_sums(k, j - 1)

    def pair_copy(k):
        return pltpu.make_async_remote_copy(
            src_ref=acc.at[k, pl.ds(TILE // 2, TILE // 2)], dst_ref=pair_in.at[k],
            send_sem=pair_s.at[k], recv_sem=pair_r.at[k],
            device_id={"prod": sibling}, device_id_type=MESH,
        )

    def y_copy(k, i):
        dy, which = cell(k, i)
        return pltpu.make_async_remote_copy(
            src_ref=acc.at[k, pl.ds(i * OWN, OWN)], dst_ref=y_in.at[which, dy - 1],
            send_sem=y_s.at[which, dy - 1], recv_sem=y_r.at[which, dy - 1],
            device_id={"prod": place(z, lax.rem(y + dy, Y), core)}, device_id_type=MESH,
        )

    def y_arrival(which, j):
        return pltpu.make_async_remote_copy(
            src_ref=z_out.at[0], dst_ref=y_in.at[which, j],
            send_sem=y_s.at[which, j], recv_sem=y_r.at[which, j],
            device_id={"prod": me}, device_id_type=MESH,
        )

    def z_copy(which, source):
        return pltpu.make_async_remote_copy(
            src_ref=z_out.at[which], dst_ref=z_in.at[source],
            send_sem=z_s.at[which], recv_sem=z_r.at[source],
            device_id={"prod": place(z_of(which), y, core)}, device_id_type=MESH,
        )

    has_next = x < x_size - 1

    def after_pair(k):
        pair_copy(k).wait_recv()
        acc[k, : TILE // 2] += pair_in[k]

        @pl.when(k >= WHOLE)
        def _():
            y_copy(k, 0).start()

        for i in (2, 1, 3):
            y_copy(k, i).start()

    def y_total(which):
        for j in range(Y - 1):
            y_arrival(which, j).wait_recv()
        whole = isinstance(which, jax.Array) or which < WHOLE
        total = acc[which, :OWN] if whole else acc[Z - 1, (which - WHOLE) * OWN : (which - WHOLE + 1) * OWN]
        for j in range(Y - 1):
            total = total + y_in[which, j]
        return total

    def after_y(which):
        z_out[which] = y_total(which)
        z_copy(which, z).start()

    last = trades // CHUNK - 1
    for k in range(EARLY):
        early_sums(k, last)
        if k == 0:
            pl.semaphore_wait(barrier, len(near) + 1 + has_next.astype(jnp.int32))
        pair_copy(k).start()

    def step(k, carry):
        acc[k] = set_sums(k, 0, trades)
        pair_copy(k).start()

        @pl.when(k == EARLY)
        def _():
            for i in range(EARLY - 1):
                after_pair(i)

        after_pair(k - 1)

        @pl.when(k >= Y_LAG)
        def _():
            after_y(k - Y_LAG)

        return carry

    lax.fori_loop(EARLY, Z, step, 0)
    for which in range(Z - Y_LAG, WHOLE):
        after_y(which)
    pair_copy(Z - 1).wait_recv()
    acc[Z - 1, : TILE // 2] += pair_in[Z - 1]
    for which in range(WHOLE, Z - 1):
        after_y(which)
    diagonal = lax.broadcasted_iota(jnp.int32, (owned, owned), 0) == lax.broadcasted_iota(
        jnp.int32, (owned, owned), 1
    )
    lag = jnp.sum(jnp.where(diagonal, lag_ref[...].astype(F32), 0.0), axis=1, keepdims=True)
    limit = jnp.sum(jnp.where(diagonal, limit_ref[...], 0.0), axis=1, keepdims=True)
    for k in range(Z):
        pair_copy(k).wait_send()
        for j in range(Y - 1):
            y_arrival(k, j).wait_send()
        if k < Z - 1:
            z_copy(k, z).wait_send()
    total = y_total(Z - 1)
    for j in range(Z):
        pl.when(j != z)(z_copy(0, j).wait_recv)
    z_in[z] = jnp.zeros_like(total)
    for j in range(Z):
        total = total + z_in[j]

    lag_out[...] = total[:, half:]
    lag_copy = pltpu.make_async_remote_copy(
        src_ref=lag_out, dst_ref=lag_in, send_sem=lag_s.at[0], recv_sem=lag_r.at[0],
        device_id={"date": x_next}, device_id_type=MESH,
    )
    pl.when(has_next)(lag_copy.start)
    pl.when(x > 0)(lag_copy.wait_recv)
    previous = jnp.where(x > 0, lag_in[...], 0.0)
    lag_one = jnp.concatenate([previous[:, paths:], total[:, : 3 * paths]], axis=1)
    lag_two = jnp.concatenate([previous, total[:, : 2 * paths]], axis=1)
    lagged = jnp.where(lag == 1.0, lag_one, jnp.where(lag == 2.0, lag_two, 0.0))
    collateral = jnp.maximum(lagged - limit, 0.0) - jnp.maximum(-lagged - limit, 0.0)
    exposure = jnp.maximum(total - collateral, 0.0)
    for d in range(dates):
        out_ref[d] = exposure[:, d * paths : (d + 1) * paths]

    pl.when(has_next)(lag_copy.wait_send)


def on_device(cash_codes, block_scales, trade_kind, strike, set_of_trade, discount, lag, limit):
    trades, buckets = cash_codes.shape
    dates, _, paths = discount.shape
    columns = dates * paths
    owned = lag.shape[0]
    live = jnp.swapaxes(discount, 1, 2).reshape(columns, buckets)
    vmem, dma = pltpu.VMEM, pltpu.SemaphoreType.DMA
    operands = (
        cash_codes, block_scales.T, trade_kind[None], strike[None], set_of_trade[None], live,
        lag[None], limit[None],
    )
    return pl.pallas_call(
        kernel,
        out_shape=jax.ShapeDtypeStruct((dates, owned, paths), F32),
        in_specs=[pl.BlockSpec(memory_space=pl.ANY)] * len(operands),
        out_specs=pl.BlockSpec(memory_space=vmem),
        scratch_shapes=[vmem(operand.shape, operand.dtype) for operand in operands]
        + [
            vmem((columns, trades), BF16),
            vmem((Z, TILE, columns), F32),
            vmem((Z, TILE // 2, columns), F32),
            vmem((Z, Y - 1, OWN, columns), F32),
            vmem((Z - 1, OWN, columns), F32),
            vmem((Z, OWN, columns), F32),
            vmem((OWN, columns // 2), F32),
            vmem((OWN, columns // 2), F32),
            dma((trades // CHUNK,)), dma((len(operands) - 1,)),
            dma((Z,)), dma((Z,)), dma((Z, Y - 1)), dma((Z, Y - 1)),
            dma((Z,)), dma((Z,)), dma((1,)), dma((1,)),
        ],
        compiler_params=pltpu.CompilerParams(
            collective_id=0, has_side_effects=True, vmem_limit_bytes=63 << 20
        ),
        name="exposure",
    )(*operands)


def solution(mesh):
    placed = (
        P("prod", None), P("prod", None), P("prod"), P("prod"), P("prod"),
        P("date", None, None), P("prod"), P("prod"),
    )
    return jax.shard_map(
        on_device, mesh=mesh, in_specs=placed, out_specs=P("date", "prod", None), check_vma=False
    )
```

```python
import functools

import jax
import jax.numpy as jnp
from jax import lax
from jax.experimental import pallas as pl
from jax.experimental.pallas import tpu as pltpu
from jax.sharding import PartitionSpec as P

MESH = pl.DeviceIdType.MESH
NT = (((1,), (1,)), ((), ()))
Z, Y, CORES = 8, 4, 2
OWN = 32
CELLS = 4
TILE = CELLS * CORES * OWN
OWN_Z = 7
TILES = (
    ((0, 0), (1, 0), (2, 0), (3, 0)),
    ((0, 1), (1, 1), (2, 1), (3, 1)),
    ((0, 2), (1, 2), (2, 2), (3, 2)),
    ((0, 3), (1, 3), (2, 3), (3, 3)),
    ((1, 4), (2, 4), (3, 4), (1, 5)),
    ((2, 5), (3, 5), (1, 6), (2, 6)),
    ((3, 6), (1, 7), (2, 7), (3, 7)),
    ((0, 4), (0, 5), (0, 6), (0, 7)),
)
CHUNKS = (2048, 2048, 2048, 2048)
Y_LAG = 5
EARLY = 2
F32, BF16 = jnp.float32, jnp.bfloat16


def place(z, y, core):
    return (z * Y + y) * CORES + core


def kernel(
    codes_hbm, scales_hbm, kind_hbm, strike_hbm, set_hbm, live_hbm, lag_hbm, limit_hbm, out_ref,
    codes, scales_ref, kind_ref, strike_ref, set_ref, live_ref, lag_ref, limit_ref,
    values, wanted, acc, pair_in, y_in, z_out, z_in, lag_out, lag_in,
    codes_sem, small_sem, pair_s, pair_r, y_s, y_r, z_s, z_r, lag_s, lag_r,
):
    trades, buckets = codes.shape
    dates, owned, paths = out_ref.shape
    columns = dates * paths
    half = columns // 2
    x = lax.axis_index("date")
    me = lax.axis_index("prod")
    core = lax.rem(me, CORES)
    y = lax.rem(me // CORES, Y)
    z = me // (CORES * Y)
    sibling = place(z, y, 1 - core)
    x_size = lax.axis_size("date")
    x_next = lax.rem(x + 1, x_size)

    small = []
    for i, (src, dst) in enumerate((
        (live_hbm, live_ref), (scales_hbm, scales_ref), (strike_hbm, strike_ref), (kind_hbm, kind_ref),
        (set_hbm, set_ref), (lag_hbm, lag_ref), (limit_hbm, limit_ref),
    )):
        small.append(pltpu.make_async_copy(src, dst, small_sem.at[i]))
    loads = []
    pieces = [pl.ds(sum(CHUNKS[:j]), count) for j, count in enumerate(CHUNKS)]
    for j, rows in enumerate(pieces):
        loads.append(pltpu.make_async_copy(codes_hbm.at[rows], codes.at[rows], codes_sem.at[j]))
    loads[0].start()
    for load in small:
        load.start()
    for load in loads[1:]:
        load.start()

    barrier = pltpu.get_barrier_semaphore()
    near = [place(z, lax.rem(y + j, Y), core) for j in range(1, Y)]
    near += [place(lax.rem(z + j, Z), y, core) for j in range(1, Z)]
    for peer in [sibling] + near:
        pl.semaphore_signal(barrier, inc=1, device_id={"prod": peer}, device_id_type=MESH)

    @pl.when(x > 0)
    def _():
        pl.semaphore_signal(barrier, inc=1, device_id={"date": x - 1}, device_id_type=MESH)

    def z_of(i):
        plain = jnp.where(i < z, i, i + 1)
        plain = jnp.where((z == 4) & (i >= 4), 11 - i, plain)
        plain = jnp.where((z == 5) & (i >= 5), 12 - i, plain)
        return jnp.where(i == Z - 1, z, plain)

    planes = [z_of(jnp.int32(i)) for i in range(Z)]
    rows_y = [lax.rem(y + dy, Y) for dy in range(Y)]

    own_row = lax.broadcasted_iota(jnp.int32, (OWN, 128), 0)
    for k, tile in enumerate(TILES):
        for i, (dy, plane) in enumerate(tile):
            for half_tile, to in enumerate((core, 1 - core)):
                row = (half_tile * CELLS + i) * OWN
                wanted[k, row : row + OWN] = (
                    own_row + place(planes[plane], rows_y[dy], to) * OWN
                ).astype(jnp.int16)

    for load in small[:4]:
        load.wait()
    total_dates = dates * x_size
    bucket = lax.broadcasted_iota(jnp.int32, (columns, buckets), 1)
    date = x * dates + lax.broadcasted_iota(jnp.int32, (columns, buckets), 0) // paths
    live = jnp.where(
        bucket >= date * (buckets // total_dates), live_ref[...].astype(F32), 0.0
    ).astype(BF16)
    blocks = scales_ref.shape[0]

    def rows_of(cell):
        k = [n for n, tile in enumerate(TILES) if cell in tile][0]
        return acc.at[k, pl.ds(TILES[k].index(cell) * OWN, OWN)]

    def set_sums(k, first, count):
        labels = jnp.concatenate([wanted[k]] * (count // 128), axis=1)
        rows = pl.ds(first, count)
        sets = set_ref[:, rows].astype(jnp.int16)
        member = jnp.where(labels == sets, BF16(1), BF16(0))
        return lax.dot_general(member, values[:, rows], NT, preferred_element_type=F32)

    def early_sums(k, j):
        part = set_sums(k, sum(CHUNKS[:j]), CHUNKS[j])
        acc[k] = part if j == 0 else acc[k] + part

    for j, rows in enumerate(pieces):
        loads[j].wait()
        code = codes[rows, :].astype(F32).astype(BF16).T.astype(F32)
        scale = scales_ref[:, rows]
        scale = jnp.concatenate(
            [jnp.broadcast_to(scale[b : b + 1], (buckets // blocks, CHUNKS[j])) for b in range(blocks)],
            axis=0,
        )
        raw = jnp.dot(live, (code * scale).astype(BF16), preferred_element_type=F32)
        floored = jnp.maximum(raw - strike_ref[:, rows], 0.0)
        values[:, rows] = jnp.where(kind_ref[:, rows] == 1, floored, raw).astype(BF16)
        if j == 0:
            for load in small[4:]:
                load.wait()
        else:
            for k in range(EARLY):
                early_sums(k, j - 1)

    def pair_copy(k):
        return pltpu.make_async_remote_copy(
            src_ref=acc.at[k, pl.ds(TILE // 2, TILE // 2)], dst_ref=pair_in.at[k],
            send_sem=pair_s.at[k], recv_sem=pair_r.at[k],
            device_id={"prod": sibling}, device_id_type=MESH,
        )

    def y_copy(dy, plane):
        return pltpu.make_async_remote_copy(
            src_ref=rows_of((dy, plane)), dst_ref=y_in.at[plane, dy - 1],
            send_sem=y_s.at[plane], recv_sem=y_r.at[plane],
            device_id={"prod": place(z, rows_y[dy], core)}, device_id_type=MESH,
        )

    def y_all(plane):
        return pltpu.make_async_remote_copy(
            src_ref=y_in.at[plane], dst_ref=y_in.at[plane],
            send_sem=y_s.at[plane], recv_sem=y_r.at[plane],
            device_id={"prod": sibling}, device_id_type=MESH,
        )

    def z_copy(plane):
        return pltpu.make_async_remote_copy(
            src_ref=z_out.at[plane], dst_ref=z_in.at[z], send_sem=z_s.at[0], recv_sem=z_r.at[0],
            device_id={"prod": place(planes[plane], y, core)}, device_id_type=MESH,
        )

    def z_all():
        return pltpu.make_async_remote_copy(
            src_ref=z_out, dst_ref=z_in.at[pl.ds(0, Z - 1)], send_sem=z_s.at[0], recv_sem=z_r.at[0],
            device_id={"prod": sibling}, device_id_type=MESH,
        )

    has_next = x < x_size - 1

    def add_pair(k):
        pair_copy(k).wait_recv()
        acc[k, : TILE // 2] += pair_in[k]

    def send_cells(k):
        for dy, plane in sorted(TILES[k], key=lambda cell: cell[0] != 2):
            if dy:
                y_copy(dy, plane).start()

    def y_total(plane):
        y_all(plane).wait_recv()
        return rows_of((0, plane))[...] + y_in[plane, 0] + y_in[plane, 1] + y_in[plane, 2]

    def after_y(plane):
        z_out[plane] = y_total(plane)
        z_copy(plane).start()

    last = len(CHUNKS) - 1
    for k in range(EARLY):
        early_sums(k, last)
        if k == 0:
            pl.semaphore_wait(barrier, len(near) + 1 + has_next.astype(jnp.int32))
        pair_copy(k).start()

    def step(k, carry):
        acc[k] = set_sums(k, 0, trades)
        pair_copy(k).start()

        @pl.when(k == EARLY)
        def _():
            for i in range(EARLY - 1):
                add_pair(i)
                send_cells(i)

        add_pair(k - 1)
        for i in range(EARLY - 1, len(TILES) - 1):
            pl.when(k == i + 1)(functools.partial(send_cells, i))
        for plane in range(len(TILES) - Y_LAG):
            pl.when(k == plane + Y_LAG)(functools.partial(after_y, plane))
        return carry

    lax.fori_loop(EARLY, len(TILES), step, 0)
    after_y(len(TILES) - Y_LAG)
    add_pair(len(TILES) - 1)
    for plane in range(len(TILES) - Y_LAG + 1, OWN_Z):
        after_y(plane)
    diagonal = lax.broadcasted_iota(jnp.int32, (owned, owned), 0) == lax.broadcasted_iota(
        jnp.int32, (owned, owned), 1
    )
    lag = jnp.sum(jnp.where(diagonal, lag_ref[...].astype(F32), 0.0), axis=1, keepdims=True)
    limit = jnp.sum(jnp.where(diagonal, limit_ref[...], 0.0), axis=1, keepdims=True)
    for k in range(len(TILES)):
        pair_copy(k).wait_send()
        y_all(k).wait_send()
    total = y_total(OWN_Z)
    z_all().wait_send()
    z_all().wait_recv()
    z_in[z] = total
    total = z_in[0]
    for j in range(1, Z):
        total = total + z_in[j]

    lag_out[...] = total[:, half:]
    lag_copy = pltpu.make_async_remote_copy(
        src_ref=lag_out, dst_ref=lag_in, send_sem=lag_s.at[0], recv_sem=lag_r.at[0],
        device_id={"date": x_next}, device_id_type=MESH,
    )
    pl.when(has_next)(lag_copy.start)
    pl.when(x > 0)(lag_copy.wait_recv)
    previous = jnp.where(x > 0, lag_in[...], 0.0)
    lag_one = jnp.concatenate([previous[:, paths:], total[:, : 3 * paths]], axis=1)
    lag_two = jnp.concatenate([previous, total[:, : 2 * paths]], axis=1)
    lagged = jnp.where(lag == 1.0, lag_one, jnp.where(lag == 2.0, lag_two, 0.0))
    collateral = jnp.maximum(lagged - limit, 0.0) - jnp.maximum(-lagged - limit, 0.0)
    exposure = jnp.maximum(total - collateral, 0.0)
    for d in range(dates):
        out_ref[d] = exposure[:, d * paths : (d + 1) * paths]

    pl.when(has_next)(lag_copy.wait_send)


def on_device(cash_codes, block_scales, trade_kind, strike, set_of_trade, discount, lag, limit):
    trades, buckets = cash_codes.shape
    dates, _, paths = discount.shape
    columns = dates * paths
    owned = lag.shape[0]
    live = jnp.swapaxes(discount, 1, 2).reshape(columns, buckets)
    vmem, dma = pltpu.VMEM, pltpu.SemaphoreType.DMA
    operands = (
        cash_codes, block_scales.T, trade_kind[None], strike[None], set_of_trade[None], live,
        lag[None], limit[None],
    )
    return pl.pallas_call(
        kernel,
        out_shape=vmem((dates, owned, paths), F32),
        in_specs=[pl.BlockSpec(memory_space=pl.ANY)] * len(operands),
        out_specs=pl.BlockSpec(memory_space=vmem),
        scratch_shapes=[vmem(operand.shape, operand.dtype) for operand in operands]
        + [
            vmem((columns, trades), BF16),
            vmem((len(TILES), TILE, 128), jnp.int16),
            vmem((Z, TILE, columns), F32),
            vmem((Z, TILE // 2, columns), F32),
            vmem((Z, Y - 1, OWN, columns), F32),
            vmem((Z - 1, OWN, columns), F32),
            vmem((Z, OWN, columns), F32),
            vmem((OWN, columns // 2), F32),
            vmem((OWN, columns // 2), F32),
            dma((len(CHUNKS),)), dma((len(operands) - 1,)),
            dma((Z,)), dma((Z,)), dma((Z,)), dma((Z,)),
            dma((1,)), dma((1,)), dma((1,)), dma((1,)),
        ],
        compiler_params=pltpu.CompilerParams(
            collective_id=0, has_side_effects=True, vmem_limit_bytes=63 << 20
        ),
        name="exposure",
    )(*operands)


def solution(mesh):
    placed = (
        P("prod", None), P("prod", None), P("prod"), P("prod"), P("prod"),
        P("date", None, None), P("prod"), P("prod"),
    )
    return jax.shard_map(
        on_device, mesh=mesh, in_specs=placed, out_specs=P("date", "prod", None), check_vma=False
    )
```

```python
import functools

import jax
import jax.numpy as jnp
from jax import lax
from jax.experimental import pallas as pl
from jax.experimental.pallas import tpu as pltpu
from jax.sharding import PartitionSpec as P

MESH = pl.DeviceIdType.MESH
NT = (((1,), (1,)), ((), ()))
Z, Y, CORES = 8, 4, 2
OWN = 32
CELLS = 4
TILE = CELLS * CORES * OWN
OWN_Z = 7
TILES = (
    ((0, 0), (1, 0), (2, 0), (3, 0)),
    ((0, 1), (1, 1), (2, 1), (3, 1)),
    ((0, 2), (1, 2), (2, 2), (3, 2)),
    ((0, 3), (1, 3), (2, 3), (3, 3)),
    ((1, 4), (2, 4), (3, 4), (1, 5)),
    ((2, 5), (3, 5), (1, 6), (2, 6)),
    ((3, 6), (1, 7), (2, 7), (3, 7)),
    ((0, 4), (0, 5), (0, 6), (0, 7)),
)
CHUNKS = (2048, 2048, 2048, 2048)
Y_LAG = 5
EARLY = 2
F32, BF16 = jnp.float32, jnp.bfloat16


def place(z, y, core):
    return (z * Y + y) * CORES + core


def kernel(
    codes_hbm, scales_hbm, kind_hbm, strike_hbm, set_hbm, live_hbm, lag_hbm, limit_hbm, out_ref,
    codes, scales_ref, kind_ref, strike_ref, set_ref, live_ref, lag_ref, limit_ref,
    values, wanted, acc, pair_in, y_in, z_out, z_in, lag_out, lag_in,
    codes_sem, small_sem, pair_s, pair_r, y_s, y_r, z_s, z_r, lag_s, lag_r,
):
    trades, buckets = codes.shape
    dates, owned, paths = out_ref.shape
    columns = dates * paths
    half = columns // 2
    x = lax.axis_index("date")
    me = lax.axis_index("prod")
    core = lax.rem(me, CORES)
    y = lax.rem(me // CORES, Y)
    z = me // (CORES * Y)
    sibling = place(z, y, 1 - core)
    x_size = lax.axis_size("date")
    x_next = lax.rem(x + 1, x_size)

    small = []
    for i, (src, dst) in enumerate((
        (live_hbm, live_ref), (scales_hbm, scales_ref), (strike_hbm, strike_ref), (kind_hbm, kind_ref),
        (set_hbm, set_ref), (lag_hbm, lag_ref), (limit_hbm, limit_ref),
    )):
        small.append(pltpu.make_async_copy(src, dst, small_sem.at[i]))
    loads = []
    pieces = [pl.ds(sum(CHUNKS[:j]), count) for j, count in enumerate(CHUNKS)]
    for j, rows in enumerate(pieces):
        loads.append(pltpu.make_async_copy(codes_hbm.at[rows], codes.at[rows], codes_sem.at[j]))
    loads[0].start()
    for load in small:
        load.start()
    for load in loads[1:]:
        load.start()

    barrier = pltpu.get_barrier_semaphore()
    near = [place(z, lax.rem(y + j, Y), core) for j in range(1, Y)]
    near += [place(lax.rem(z + j, Z), y, core) for j in range(1, Z)]
    for peer in [sibling] + near:
        pl.semaphore_signal(barrier, inc=1, device_id={"prod": peer}, device_id_type=MESH)

    @pl.when(x > 0)
    def _():
        pl.semaphore_signal(barrier, inc=1, device_id={"date": x - 1}, device_id_type=MESH)

    def z_of(i):
        plain = jnp.where(i < z, i, i + 1)
        plain = jnp.where((z == 4) & (i >= 4), 11 - i, plain)
        plain = jnp.where((z == 5) & (i >= 5), 12 - i, plain)
        return jnp.where(i == Z - 1, z, plain)

    planes = [z_of(jnp.int32(i)) for i in range(Z)]
    rows_y = [lax.rem(y + dy, Y) for dy in range(Y)]

    own_row = lax.broadcasted_iota(jnp.int32, (OWN, 128), 0)
    for k, tile in enumerate(TILES):
        for i, (dy, plane) in enumerate(tile):
            for half_tile, to in enumerate((core, 1 - core)):
                row = (half_tile * CELLS + i) * OWN
                wanted[k, row : row + OWN] = (
                    own_row + place(planes[plane], rows_y[dy], to) * OWN
                ).astype(jnp.int16)

    for load in small[:4]:
        load.wait()
    total_dates = dates * x_size
    bucket = lax.broadcasted_iota(jnp.int32, (columns, buckets), 1)
    date = x * dates + lax.broadcasted_iota(jnp.int32, (columns, buckets), 0) // paths
    live = jnp.where(
        bucket >= date * (buckets // total_dates), live_ref[...].astype(F32), 0.0
    ).astype(BF16)
    blocks = scales_ref.shape[0]

    def rows_of(cell):
        k = [n for n, tile in enumerate(TILES) if cell in tile][0]
        return acc.at[k, pl.ds(TILES[k].index(cell) * OWN, OWN)]

    def set_sums(k, first, count):
        labels = jnp.concatenate([wanted[k]] * (count // 128), axis=1)
        rows = pl.ds(first, count)
        sets = set_ref[:, rows].astype(jnp.int16)
        member = jnp.where(labels == sets, BF16(1), BF16(0))
        return lax.dot_general(member, values[:, rows], NT, preferred_element_type=F32)

    def early_sums(k, j):
        part = set_sums(k, sum(CHUNKS[:j]), CHUNKS[j])
        acc[k] = part if j == 0 else acc[k] + part

    for j, rows in enumerate(pieces):
        loads[j].wait()
        code = codes[rows, :].astype(F32).astype(BF16).T.astype(F32)
        scale = scales_ref[:, rows]
        scale = jnp.concatenate(
            [jnp.broadcast_to(scale[b : b + 1], (buckets // blocks, CHUNKS[j])) for b in range(blocks)],
            axis=0,
        )
        raw = jnp.dot(live, (code * scale).astype(BF16), preferred_element_type=F32)
        floored = jnp.maximum(raw - strike_ref[:, rows], 0.0)
        values[:, rows] = jnp.where(kind_ref[:, rows] == 1, floored, raw).astype(BF16)
        if j == 0:
            for load in small[4:]:
                load.wait()
        else:
            for k in range(EARLY):
                early_sums(k, j - 1)

    def pair_copy(k):
        return pltpu.make_async_remote_copy(
            src_ref=acc.at[k, pl.ds(TILE // 2, TILE // 2)], dst_ref=pair_in.at[k],
            send_sem=pair_s.at[k], recv_sem=pair_r.at[k],
            device_id={"prod": sibling}, device_id_type=MESH,
        )

    def y_copy(dy, plane):
        return pltpu.make_async_remote_copy(
            src_ref=rows_of((dy, plane)), dst_ref=y_in.at[plane, dy - 1],
            send_sem=y_s.at[plane], recv_sem=y_r.at[plane],
            device_id={"prod": place(z, rows_y[dy], core)}, device_id_type=MESH,
        )

    def y_all(plane):
        return pltpu.make_async_remote_copy(
            src_ref=y_in.at[plane], dst_ref=y_in.at[plane],
            send_sem=y_s.at[plane], recv_sem=y_r.at[plane],
            device_id={"prod": sibling}, device_id_type=MESH,
        )

    def z_copy(plane):
        return pltpu.make_async_remote_copy(
            src_ref=z_out.at[plane], dst_ref=z_in.at[z], send_sem=z_s.at[0], recv_sem=z_r.at[0],
            device_id={"prod": place(planes[plane], y, core)}, device_id_type=MESH,
        )

    def z_all():
        return pltpu.make_async_remote_copy(
            src_ref=z_out, dst_ref=z_in.at[pl.ds(0, Z - 1)], send_sem=z_s.at[0], recv_sem=z_r.at[0],
            device_id={"prod": sibling}, device_id_type=MESH,
        )

    has_next = x < x_size - 1

    def add_pair(k):
        pair_copy(k).wait_recv()
        acc[k, : TILE // 2] += pair_in[k]

    def send_cells(k):
        for dy, plane in TILES[k]:
            if dy:
                y_copy(dy, plane).start()

    def y_total(plane):
        y_all(plane).wait_recv()
        return rows_of((0, plane))[...] + y_in[plane, 0] + y_in[plane, 1] + y_in[plane, 2]

    def after_y(plane):
        z_out[plane] = y_total(plane)
        z_copy(plane).start()

    last = len(CHUNKS) - 1
    for k in range(EARLY):
        early_sums(k, last)
        if k == 0:
            pl.semaphore_wait(barrier, len(near) + 1 + has_next.astype(jnp.int32))
        pair_copy(k).start()

    def step(k, carry):
        acc[k] = set_sums(k, 0, trades)
        pair_copy(k).start()

        @pl.when(k == EARLY)
        def _():
            for i in range(EARLY - 1):
                add_pair(i)
                send_cells(i)

        add_pair(k - 1)
        for i in range(EARLY - 1, len(TILES) - 1):
            pl.when(k == i + 1)(functools.partial(send_cells, i))
        for plane in range(len(TILES) - Y_LAG):
            pl.when(k == plane + Y_LAG)(functools.partial(after_y, plane))
        return carry

    lax.fori_loop(EARLY, len(TILES), step, 0)
    after_y(len(TILES) - Y_LAG)
    add_pair(len(TILES) - 1)
    for plane in range(len(TILES) - Y_LAG + 1, OWN_Z):
        after_y(plane)
    diagonal = lax.broadcasted_iota(jnp.int32, (owned, owned), 0) == lax.broadcasted_iota(
        jnp.int32, (owned, owned), 1
    )
    lag = jnp.sum(jnp.where(diagonal, lag_ref[...].astype(F32), 0.0), axis=1, keepdims=True)
    limit = jnp.sum(jnp.where(diagonal, limit_ref[...], 0.0), axis=1, keepdims=True)
    for k in range(len(TILES)):
        pair_copy(k).wait_send()
        y_all(k).wait_send()
    total = y_total(OWN_Z)
    z_all().wait_send()
    z_all().wait_recv()
    z_in[z] = total
    total = z_in[0]
    for j in range(1, Z):
        total = total + z_in[j]

    lag_out[...] = total[:, half:]
    lag_copy = pltpu.make_async_remote_copy(
        src_ref=lag_out, dst_ref=lag_in, send_sem=lag_s.at[0], recv_sem=lag_r.at[0],
        device_id={"date": x_next}, device_id_type=MESH,
    )
    pl.when(has_next)(lag_copy.start)
    pl.when(x > 0)(lag_copy.wait_recv)
    previous = jnp.where(x > 0, lag_in[...], 0.0)
    lag_one = jnp.concatenate([previous[:, paths:], total[:, : 3 * paths]], axis=1)
    lag_two = jnp.concatenate([previous, total[:, : 2 * paths]], axis=1)
    lagged = jnp.where(lag == 1.0, lag_one, jnp.where(lag == 2.0, lag_two, 0.0))
    collateral = jnp.maximum(lagged - limit, 0.0) - jnp.maximum(-lagged - limit, 0.0)
    exposure = jnp.maximum(total - collateral, 0.0)
    for d in range(dates):
        out_ref[d] = exposure[:, d * paths : (d + 1) * paths]

    pl.when(has_next)(lag_copy.wait_send)


def on_device(cash_codes, block_scales, trade_kind, strike, set_of_trade, discount, lag, limit):
    trades, buckets = cash_codes.shape
    dates, _, paths = discount.shape
    columns = dates * paths
    owned = lag.shape[0]
    live = jnp.swapaxes(discount, 1, 2).reshape(columns, buckets)
    vmem, dma = pltpu.VMEM, pltpu.SemaphoreType.DMA
    operands = (
        cash_codes, block_scales.T, trade_kind[None], strike[None], set_of_trade[None], live,
        lag[None], limit[None],
    )
    return pl.pallas_call(
        kernel,
        out_shape=vmem((dates, owned, paths), F32),
        in_specs=[pl.BlockSpec(memory_space=pl.ANY)] * len(operands),
        out_specs=pl.BlockSpec(memory_space=vmem),
        scratch_shapes=[vmem(operand.shape, operand.dtype) for operand in operands]
        + [
            vmem((columns, trades), BF16),
            vmem((len(TILES), TILE, 128), jnp.int16),
            vmem((Z, TILE, columns), F32),
            vmem((Z, TILE // 2, columns), F32),
            vmem((Z, Y - 1, OWN, columns), F32),
            vmem((Z - 1, OWN, columns), F32),
            vmem((Z, OWN, columns), F32),
            vmem((OWN, columns // 2), F32),
            vmem((OWN, columns // 2), F32),
            dma((len(CHUNKS),)), dma((len(operands) - 1,)),
            dma((Z,)), dma((Z,)), dma((Z,)), dma((Z,)),
            dma((1,)), dma((1,)), dma((1,)), dma((1,)),
        ],
        compiler_params=pltpu.CompilerParams(
            collective_id=0, has_side_effects=True, vmem_limit_bytes=63 << 20
        ),
        name="exposure",
    )(*operands)


def solution(mesh):
    placed = (
        P("prod", None), P("prod", None), P("prod"), P("prod"), P("prod"),
        P("date", None, None), P("prod"), P("prod"),
    )
    return jax.shard_map(
        on_device, mesh=mesh, in_specs=placed, out_specs=P("date", "prod", None), check_vma=False
    )
```

```python
import functools

import jax
import jax.numpy as jnp
from jax import lax
from jax.experimental import pallas as pl
from jax.experimental.pallas import tpu as pltpu
from jax.sharding import PartitionSpec as P

MESH = pl.DeviceIdType.MESH
NT = (((1,), (1,)), ((), ()))
Z, Y, CORES = 8, 4, 2
OWN = 32
CELLS = 4
TILE = CELLS * CORES * OWN
OWN_Z = 7
TILES = (
    ((0, 0), (1, 0), (2, 0), (3, 0)),
    ((0, 1), (1, 1), (2, 1), (3, 1)),
    ((0, 2), (1, 2), (2, 2), (3, 2)),
    ((0, 3), (1, 3), (2, 3), (3, 3)),
    ((1, 4), (2, 4), (3, 4), (1, 5)),
    ((2, 5), (3, 5), (1, 6), (2, 6)),
    ((3, 6), (1, 7), (2, 7), (3, 7)),
    ((0, 4), (0, 5), (0, 6), (0, 7)),
)
CHUNKS = (1024, 1024, 2048, 2048, 2048)
Y_LAG = 5
EARLY = 2
F32, BF16 = jnp.float32, jnp.bfloat16


def place(z, y, core):
    return (z * Y + y) * CORES + core


def kernel(
    codes_hbm, scales_hbm, kind_hbm, strike_hbm, set_hbm, live_hbm, lag_hbm, limit_hbm, out_ref,
    codes, scales_ref, kind_ref, strike_ref, set_ref, live_ref, lag_ref, limit_ref,
    values, wanted, acc, pair_in, y_in, z_out, z_in, lag_out, lag_in,
    codes_sem, small_sem, pair_s, pair_r, y_s, y_r, z_s, z_r, lag_s, lag_r,
):
    trades, buckets = codes.shape
    dates, owned, paths = out_ref.shape
    columns = dates * paths
    half = columns // 2
    x = lax.axis_index("date")
    me = lax.axis_index("prod")
    core = lax.rem(me, CORES)
    y = lax.rem(me // CORES, Y)
    z = me // (CORES * Y)
    sibling = place(z, y, 1 - core)
    x_size = lax.axis_size("date")
    x_next = lax.rem(x + 1, x_size)

    small = []
    for i, (src, dst) in enumerate((
        (live_hbm, live_ref), (scales_hbm, scales_ref), (strike_hbm, strike_ref), (kind_hbm, kind_ref),
        (set_hbm, set_ref), (lag_hbm, lag_ref), (limit_hbm, limit_ref),
    )):
        small.append(pltpu.make_async_copy(src, dst, small_sem.at[i]))
    loads = []
    pieces = [pl.ds(sum(CHUNKS[:j]), count) for j, count in enumerate(CHUNKS)]
    for j, rows in enumerate(pieces):
        loads.append(pltpu.make_async_copy(codes_hbm.at[rows], codes.at[rows], codes_sem.at[j]))
    loads[0].start()
    for load in small:
        load.start()
    for load in loads[1:]:
        load.start()

    barrier = pltpu.get_barrier_semaphore()
    near = [place(z, lax.rem(y + j, Y), core) for j in range(1, Y)]
    near += [place(lax.rem(z + j, Z), y, core) for j in range(1, Z)]
    for peer in [sibling] + near:
        pl.semaphore_signal(barrier, inc=1, device_id={"prod": peer}, device_id_type=MESH)

    @pl.when(x > 0)
    def _():
        pl.semaphore_signal(barrier, inc=1, device_id={"date": x - 1}, device_id_type=MESH)

    def z_of(i):
        plain = jnp.where(i < z, i, i + 1)
        plain = jnp.where((z == 4) & (i >= 4), 11 - i, plain)
        plain = jnp.where((z == 5) & (i >= 5), 12 - i, plain)
        return jnp.where(i == Z - 1, z, plain)

    planes = [z_of(jnp.int32(i)) for i in range(Z)]
    rows_y = [lax.rem(y + dy, Y) for dy in range(Y)]

    own_row = lax.broadcasted_iota(jnp.int32, (OWN, 128), 0)
    for k, tile in enumerate(TILES):
        for i, (dy, plane) in enumerate(tile):
            for half_tile, to in enumerate((core, 1 - core)):
                row = (half_tile * CELLS + i) * OWN
                wanted[k, row : row + OWN] = (
                    own_row + place(planes[plane], rows_y[dy], to) * OWN
                ).astype(jnp.int16)

    for load in small[:4]:
        load.wait()
    total_dates = dates * x_size
    bucket = lax.broadcasted_iota(jnp.int32, (columns, buckets), 1)
    date = x * dates + lax.broadcasted_iota(jnp.int32, (columns, buckets), 0) // paths
    live = jnp.where(
        bucket >= date * (buckets // total_dates), live_ref[...].astype(F32), 0.0
    ).astype(BF16)
    blocks = scales_ref.shape[0]

    def rows_of(cell):
        k = [n for n, tile in enumerate(TILES) if cell in tile][0]
        return acc.at[k, pl.ds(TILES[k].index(cell) * OWN, OWN)]

    def set_sums(k, first, count):
        labels = jnp.concatenate([wanted[k]] * (count // 128), axis=1)
        rows = pl.ds(first, count)
        sets = set_ref[:, rows].astype(jnp.int16)
        member = jnp.where(labels == sets, BF16(1), BF16(0))
        return lax.dot_general(member, values[:, rows], NT, preferred_element_type=F32)

    def early_sums(k, j):
        part = set_sums(k, sum(CHUNKS[:j]), CHUNKS[j])
        acc[k] = part if j == 0 else acc[k] + part

    for j, rows in enumerate(pieces):
        if j < 2:
            loads[j].wait()
        elif j == 2:
            for load in loads[2:]:
                load.wait()
        code = codes[rows, :].astype(F32).astype(BF16).T.astype(F32)
        scale = scales_ref[:, rows]
        scale = jnp.concatenate(
            [jnp.broadcast_to(scale[b : b + 1], (buckets // blocks, CHUNKS[j])) for b in range(blocks)],
            axis=0,
        )
        raw = jnp.dot(live, (code * scale).astype(BF16), preferred_element_type=F32)
        floored = jnp.maximum(raw - strike_ref[:, rows], 0.0)
        values[:, rows] = jnp.where(kind_ref[:, rows] == 1, floored, raw).astype(BF16)
        if j == 0:
            for load in small[4:]:
                load.wait()
        else:
            for k in range(EARLY):
                early_sums(k, j - 1)

    def pair_copy(k):
        return pltpu.make_async_remote_copy(
            src_ref=acc.at[k, pl.ds(TILE // 2, TILE // 2)], dst_ref=pair_in.at[k],
            send_sem=pair_s.at[k], recv_sem=pair_r.at[k],
            device_id={"prod": sibling}, device_id_type=MESH,
        )

    def y_copy(dy, plane):
        return pltpu.make_async_remote_copy(
            src_ref=rows_of((dy, plane)), dst_ref=y_in.at[plane, dy - 1],
            send_sem=y_s.at[plane], recv_sem=y_r.at[plane],
            device_id={"prod": place(z, rows_y[dy], core)}, device_id_type=MESH,
        )

    def y_all(plane):
        return pltpu.make_async_remote_copy(
            src_ref=y_in.at[plane], dst_ref=y_in.at[plane],
            send_sem=y_s.at[plane], recv_sem=y_r.at[plane],
            device_id={"prod": sibling}, device_id_type=MESH,
        )

    def z_copy(plane):
        return pltpu.make_async_remote_copy(
            src_ref=z_out.at[plane], dst_ref=z_in.at[z], send_sem=z_s.at[0], recv_sem=z_r.at[0],
            device_id={"prod": place(planes[plane], y, core)}, device_id_type=MESH,
        )

    def z_all():
        return pltpu.make_async_remote_copy(
            src_ref=z_out, dst_ref=z_in.at[pl.ds(0, Z - 1)], send_sem=z_s.at[0], recv_sem=z_r.at[0],
            device_id={"prod": sibling}, device_id_type=MESH,
        )

    has_next = x < x_size - 1

    def add_pair(k):
        pair_copy(k).wait_recv()
        acc[k, : TILE // 2] += pair_in[k]

    def send_cells(k):
        for dy, plane in TILES[k]:
            if dy:
                y_copy(dy, plane).start()

    def y_total(plane):
        y_all(plane).wait_recv()
        return rows_of((0, plane))[...] + y_in[plane, 0] + y_in[plane, 1] + y_in[plane, 2]

    def after_y(plane):
        z_out[plane] = y_total(plane)
        z_copy(plane).start()

    last = len(CHUNKS) - 1
    for k in range(EARLY):
        early_sums(k, last)
        if k == 0:
            pl.semaphore_wait(barrier, len(near) + 1 + has_next.astype(jnp.int32))
        pair_copy(k).start()

    def step(k, carry):
        acc[k] = set_sums(k, 0, trades)
        pair_copy(k).start()

        @pl.when(k == EARLY)
        def _():
            for i in range(EARLY - 1):
                add_pair(i)
                send_cells(i)

        add_pair(k - 1)
        for i in range(EARLY - 1, len(TILES) - 1):
            pl.when(k == i + 1)(functools.partial(send_cells, i))
        pl.when(k == 5)(functools.partial(after_y, 0))
        pl.when(k == 6)(functools.partial(after_y, 1))
        return carry

    lax.fori_loop(EARLY, len(TILES), step, 0)
    after_y(2)
    after_y(3)
    add_pair(len(TILES) - 1)
    for plane in range(len(TILES) - Y_LAG + 1, OWN_Z):
        after_y(plane)
    diagonal = lax.broadcasted_iota(jnp.int32, (owned, owned), 0) == lax.broadcasted_iota(
        jnp.int32, (owned, owned), 1
    )
    lag = jnp.sum(jnp.where(diagonal, lag_ref[...].astype(F32), 0.0), axis=1, keepdims=True)
    limit = jnp.sum(jnp.where(diagonal, limit_ref[...], 0.0), axis=1, keepdims=True)
    total = y_total(OWN_Z)
    z_all().wait_recv()
    z_in[z] = total
    ahead = z_in[0, :, half:]
    for j in range(1, Z):
        ahead = ahead + z_in[j, :, half:]
    lag_out[...] = ahead

    lag_copy = pltpu.make_async_remote_copy(
        src_ref=lag_out, dst_ref=lag_in, send_sem=lag_s.at[0], recv_sem=lag_r.at[0],
        device_id={"date": x_next}, device_id_type=MESH,
    )
    pl.when(has_next)(lag_copy.start)
    total = z_in[0]
    for j in range(1, Z):
        total = total + z_in[j]
    pl.when(x > 0)(lag_copy.wait_recv)
    previous = jnp.where(x > 0, lag_in[...], 0.0)
    lag_one = jnp.concatenate([previous[:, paths:], total[:, : 3 * paths]], axis=1)
    lag_two = jnp.concatenate([previous, total[:, : 2 * paths]], axis=1)
    lagged = jnp.where(lag == 1.0, lag_one, jnp.where(lag == 2.0, lag_two, 0.0))
    collateral = jnp.maximum(lagged - limit, 0.0) - jnp.maximum(-lagged - limit, 0.0)
    exposure = jnp.maximum(total - collateral, 0.0)
    for d in range(dates):
        out_ref[d] = exposure[:, d * paths : (d + 1) * paths]

    for k in range(len(TILES)):
        pair_copy(k).wait_send()
        y_all(k).wait_send()
    z_all().wait_send()
    pl.when(has_next)(lag_copy.wait_send)


def on_device(cash_codes, block_scales, trade_kind, strike, set_of_trade, discount, lag, limit):
    trades, buckets = cash_codes.shape
    dates, _, paths = discount.shape
    columns = dates * paths
    owned = lag.shape[0]
    live = jnp.swapaxes(discount, 1, 2).reshape(columns, buckets)
    vmem, dma = pltpu.VMEM, pltpu.SemaphoreType.DMA
    operands = (
        cash_codes, block_scales.T, trade_kind[None], strike[None], set_of_trade[None], live,
        lag[None], limit[None],
    )
    return pl.pallas_call(
        kernel,
        out_shape=vmem((dates, owned, paths), F32),
        in_specs=[pl.BlockSpec(memory_space=pl.ANY)] * len(operands),
        out_specs=pl.BlockSpec(memory_space=vmem),
        scratch_shapes=[vmem(operand.shape, operand.dtype) for operand in operands]
        + [
            vmem((columns, trades), BF16),
            vmem((len(TILES), TILE, 128), jnp.int16),
            vmem((Z, TILE, columns), F32),
            vmem((Z, TILE // 2, columns), F32),
            vmem((Z, Y - 1, OWN, columns), F32),
            vmem((Z - 1, OWN, columns), F32),
            vmem((Z, OWN, columns), F32),
            vmem((OWN, columns // 2), F32),
            vmem((OWN, columns // 2), F32),
            dma((len(CHUNKS),)), dma((len(operands) - 1,)),
            dma((Z,)), dma((Z,)), dma((Z,)), dma((Z,)),
            dma((1,)), dma((1,)), dma((1,)), dma((1,)),
        ],
        compiler_params=pltpu.CompilerParams(
            collective_id=0, has_side_effects=True, vmem_limit_bytes=63 << 20
        ),
        name="exposure",
    )(*operands)


def solution(mesh):
    placed = (
        P("prod", None), P("prod", None), P("prod"), P("prod"), P("prod"),
        P("date", None, None), P("prod"), P("prod"),
    )
    return jax.shard_map(
        on_device, mesh=mesh, in_specs=placed, out_specs=P("date", "prod", None), check_vma=False
    )
```

```python
import functools

import jax
import jax.numpy as jnp
from jax import lax
from jax.experimental import pallas as pl
from jax.experimental.pallas import tpu as pltpu
from jax.sharding import PartitionSpec as P

MESH = pl.DeviceIdType.MESH
NT = (((1,), (1,)), ((), ()))
Z, Y, CORES = 8, 4, 2
OWN = 32
CELLS = 4
TILE = CELLS * CORES * OWN
OWN_Z = 7
TILES = (
    ((0, 0), (1, 0), (2, 0), (3, 0)),
    ((0, 1), (1, 1), (2, 1), (3, 1)),
    ((0, 2), (1, 2), (2, 2), (3, 2)),
    ((0, 3), (1, 3), (2, 3), (3, 3)),
    ((1, 4), (2, 4), (3, 4), (1, 5)),
    ((2, 5), (3, 5), (1, 6), (2, 6)),
    ((3, 6), (1, 7), (2, 7), (3, 7)),
    ((0, 4), (0, 5), (0, 6), (0, 7)),
)
CHUNKS = (2048, 2048, 2048, 2048)
Y_LAG = 5
EARLY = 2
F32, BF16 = jnp.float32, jnp.bfloat16


def place(z, y, core):
    return (z * Y + y) * CORES + core


def kernel(
    codes_hbm, scales_hbm, kind_hbm, strike_hbm, set_hbm, live_hbm, lag_hbm, limit_hbm, out_ref,
    codes, scales_ref, kind_ref, strike_ref, set_ref, live_ref, lag_ref, limit_ref,
    values, wanted, acc, pair_in, y_in, z_out, z_in, lag_out, lag_in,
    codes_sem, small_sem, pair_s, pair_r, y_s, y_r, z_s, z_r, lag_s, lag_r,
):
    trades, buckets = codes.shape
    dates, owned, paths = out_ref.shape
    columns = dates * paths
    half = columns // 2
    x = lax.axis_index("date")
    me = lax.axis_index("prod")
    core = lax.rem(me, CORES)
    y = lax.rem(me // CORES, Y)
    z = me // (CORES * Y)
    sibling = place(z, y, 1 - core)
    x_size = lax.axis_size("date")
    x_next = lax.rem(x + 1, x_size)

    small = []
    for i, (src, dst) in enumerate((
        (live_hbm, live_ref), (scales_hbm, scales_ref), (strike_hbm, strike_ref), (kind_hbm, kind_ref),
        (set_hbm, set_ref), (lag_hbm, lag_ref), (limit_hbm, limit_ref),
    )):
        small.append(pltpu.make_async_copy(src, dst, small_sem.at[i]))
    loads = []
    pieces = [pl.ds(sum(CHUNKS[:j]), count) for j, count in enumerate(CHUNKS)]
    for j, rows in enumerate(pieces):
        loads.append(pltpu.make_async_copy(codes_hbm.at[rows], codes.at[rows], codes_sem.at[j]))
    loads[0].start()
    for load in small:
        load.start()
    for load in loads[1:]:
        load.start()

    barrier = pltpu.get_barrier_semaphore()
    near = [place(z, lax.rem(y + j, Y), core) for j in range(1, Y)]
    near += [place(lax.rem(z + j, Z), y, core) for j in range(1, Z)]
    for peer in [sibling] + near:
        pl.semaphore_signal(barrier, inc=1, device_id={"prod": peer}, device_id_type=MESH)

    @pl.when(x > 0)
    def _():
        pl.semaphore_signal(barrier, inc=1, device_id={"date": x - 1}, device_id_type=MESH)

    def z_of(i):
        plain = jnp.where(i < z, i, i + 1)
        plain = jnp.where((z == 4) & (i >= 4), 11 - i, plain)
        plain = jnp.where((z == 5) & (i >= 5), 12 - i, plain)
        return jnp.where(i == Z - 1, z, plain)

    planes = [z_of(jnp.int32(i)) for i in range(Z)]
    rows_y = [lax.rem(y + dy, Y) for dy in range(Y)]

    own_row = lax.broadcasted_iota(jnp.int32, (OWN, 128), 0)
    for k, tile in enumerate(TILES):
        for i, (dy, plane) in enumerate(tile):
            for half_tile, to in enumerate((core, 1 - core)):
                row = (half_tile * CELLS + i) * OWN
                wanted[k, row : row + OWN] = (
                    own_row + place(planes[plane], rows_y[dy], to) * OWN
                ).astype(jnp.int16)

    for load in small[:4]:
        load.wait()
    total_dates = dates * x_size
    bucket = lax.broadcasted_iota(jnp.int32, (columns, buckets), 1)
    date = x * dates + lax.broadcasted_iota(jnp.int32, (columns, buckets), 0) // paths
    live = jnp.where(
        bucket >= date * (buckets // total_dates), live_ref[...].astype(F32), 0.0
    ).astype(BF16)
    blocks = scales_ref.shape[0]

    def rows_of(cell):
        k = [n for n, tile in enumerate(TILES) if cell in tile][0]
        return acc.at[k, pl.ds(TILES[k].index(cell) * OWN, OWN)]

    def set_sums(k, first, count):
        labels = jnp.concatenate([wanted[k]] * (count // 128), axis=1)
        rows = pl.ds(first, count)
        sets = set_ref[:, rows].astype(jnp.int16)
        member = jnp.where(labels == sets, BF16(1), BF16(0))
        return lax.dot_general(member, values[:, rows], NT, preferred_element_type=F32)

    def early_sums(k, j):
        part = set_sums(k, sum(CHUNKS[:j]), CHUNKS[j])
        acc[k] = part if j == 0 else acc[k] + part

    for j, rows in enumerate(pieces):
        loads[j].wait()
        code = codes[rows, :].astype(F32).astype(BF16).T.astype(F32)
        scale = scales_ref[:, rows]
        scale = jnp.concatenate(
            [jnp.broadcast_to(scale[b : b + 1], (buckets // blocks, CHUNKS[j])) for b in range(blocks)],
            axis=0,
        )
        raw = jnp.dot(live, (code * scale).astype(BF16), preferred_element_type=F32)
        floored = jnp.maximum(raw - strike_ref[:, rows], 0.0)
        values[:, rows] = jnp.where(kind_ref[:, rows] == 1, floored, raw).astype(BF16)
        if j == 0:
            for load in small[4:]:
                load.wait()
        else:
            for k in range(EARLY):
                early_sums(k, j - 1)

    def pair_copy(k):
        return pltpu.make_async_remote_copy(
            src_ref=acc.at[k, pl.ds(TILE // 2, TILE // 2)], dst_ref=pair_in.at[k],
            send_sem=pair_s.at[k], recv_sem=pair_r.at[k],
            device_id={"prod": sibling}, device_id_type=MESH,
        )

    def y_copy(dy, plane):
        return pltpu.make_async_remote_copy(
            src_ref=rows_of((dy, plane)), dst_ref=y_in.at[plane, dy - 1],
            send_sem=y_s.at[plane], recv_sem=y_r.at[plane],
            device_id={"prod": place(z, rows_y[dy], core)}, device_id_type=MESH,
        )

    def y_all(plane):
        return pltpu.make_async_remote_copy(
            src_ref=y_in.at[plane], dst_ref=y_in.at[plane],
            send_sem=y_s.at[plane], recv_sem=y_r.at[plane],
            device_id={"prod": sibling}, device_id_type=MESH,
        )

    def z_copy(plane):
        return pltpu.make_async_remote_copy(
            src_ref=z_out.at[plane], dst_ref=z_in.at[z], send_sem=z_s.at[0], recv_sem=z_r.at[0],
            device_id={"prod": place(planes[plane], y, core)}, device_id_type=MESH,
        )

    def z_all():
        return pltpu.make_async_remote_copy(
            src_ref=z_out, dst_ref=z_in.at[pl.ds(0, Z - 1)], send_sem=z_s.at[0], recv_sem=z_r.at[0],
            device_id={"prod": sibling}, device_id_type=MESH,
        )

    has_next = x < x_size - 1

    def add_pair(k):
        pair_copy(k).wait_recv()
        acc[k, : TILE // 2] += pair_in[k]

    def send_cells(k):
        for dy, plane in TILES[k]:
            if dy:
                y_copy(dy, plane).start()

    def y_total(plane):
        y_all(plane).wait_recv()
        return rows_of((0, plane))[...] + y_in[plane, 0] + y_in[plane, 1] + y_in[plane, 2]

    def after_y(plane):
        z_out[plane] = y_total(plane)
        z_copy(plane).start()

    last = len(CHUNKS) - 1
    for k in range(EARLY):
        early_sums(k, last)
        if k == 0:
            pl.semaphore_wait(barrier, len(near) + 1 + has_next.astype(jnp.int32))
        pair_copy(k).start()

    def step(k, carry):
        acc[k] = set_sums(k, 0, trades)
        pair_copy(k).start()

        @pl.when(k == EARLY)
        def _():
            for i in range(EARLY - 1):
                add_pair(i)
                send_cells(i)

        add_pair(k - 1)
        for i in range(EARLY - 1, len(TILES) - 1):
            pl.when(k == i + 1)(functools.partial(send_cells, i))
        pl.when(k == 6)(functools.partial(after_y, 0))
        pl.when(k == 6)(functools.partial(after_y, 1))
        pl.when(k == 7)(functools.partial(after_y, 2))
        return carry

    lax.fori_loop(EARLY, len(TILES), step, 0)
    after_y(3)
    add_pair(len(TILES) - 1)
    for plane in range(len(TILES) - Y_LAG + 1, OWN_Z):
        after_y(plane)
    diagonal = lax.broadcasted_iota(jnp.int32, (owned, owned), 0) == lax.broadcasted_iota(
        jnp.int32, (owned, owned), 1
    )
    lag = jnp.sum(jnp.where(diagonal, lag_ref[...].astype(F32), 0.0), axis=1, keepdims=True)
    limit = jnp.sum(jnp.where(diagonal, limit_ref[...], 0.0), axis=1, keepdims=True)
    for k in range(len(TILES)):
        pair_copy(k).wait_send()
        y_all(k).wait_send()
    total = y_total(OWN_Z)
    z_all().wait_send()
    z_all().wait_recv()
    z_in[z] = total
    total = z_in[0]
    for j in range(1, Z):
        total = total + z_in[j]

    lag_out[...] = total[:, half:]
    lag_copy = pltpu.make_async_remote_copy(
        src_ref=lag_out, dst_ref=lag_in, send_sem=lag_s.at[0], recv_sem=lag_r.at[0],
        device_id={"date": x_next}, device_id_type=MESH,
    )
    pl.when(has_next)(lag_copy.start)
    pl.when(x > 0)(lag_copy.wait_recv)
    previous = jnp.where(x > 0, lag_in[...], 0.0)
    lag_one = jnp.concatenate([previous[:, paths:], total[:, : 3 * paths]], axis=1)
    lag_two = jnp.concatenate([previous, total[:, : 2 * paths]], axis=1)
    lagged = jnp.where(lag == 1.0, lag_one, jnp.where(lag == 2.0, lag_two, 0.0))
    collateral = jnp.maximum(lagged - limit, 0.0) - jnp.maximum(-lagged - limit, 0.0)
    exposure = jnp.maximum(total - collateral, 0.0)
    for d in range(dates):
        out_ref[d] = exposure[:, d * paths : (d + 1) * paths]

    pl.when(has_next)(lag_copy.wait_send)


def on_device(cash_codes, block_scales, trade_kind, strike, set_of_trade, discount, lag, limit):
    trades, buckets = cash_codes.shape
    dates, _, paths = discount.shape
    columns = dates * paths
    owned = lag.shape[0]
    live = jnp.swapaxes(discount, 1, 2).reshape(columns, buckets)
    vmem, dma = pltpu.VMEM, pltpu.SemaphoreType.DMA
    operands = (
        cash_codes, block_scales.T, trade_kind[None], strike[None], set_of_trade[None], live,
        lag[None], limit[None],
    )
    return pl.pallas_call(
        kernel,
        out_shape=vmem((dates, owned, paths), F32),
        in_specs=[pl.BlockSpec(memory_space=pl.ANY)] * len(operands),
        out_specs=pl.BlockSpec(memory_space=vmem),
        scratch_shapes=[vmem(operand.shape, operand.dtype) for operand in operands]
        + [
            vmem((columns, trades), BF16),
            vmem((len(TILES), TILE, 128), jnp.int16),
            vmem((Z, TILE, columns), F32),
            vmem((Z, TILE // 2, columns), F32),
            vmem((Z, Y - 1, OWN, columns), F32),
            vmem((Z - 1, OWN, columns), F32),
            vmem((Z, OWN, columns), F32),
            vmem((OWN, columns // 2), F32),
            vmem((OWN, columns // 2), F32),
            dma((len(CHUNKS),)), dma((len(operands) - 1,)),
            dma((Z,)), dma((Z,)), dma((Z,)), dma((Z,)),
            dma((1,)), dma((1,)), dma((1,)), dma((1,)),
        ],
        compiler_params=pltpu.CompilerParams(
            collective_id=0, has_side_effects=True, vmem_limit_bytes=63 << 20
        ),
        name="exposure",
    )(*operands)


def solution(mesh):
    placed = (
        P("prod", None), P("prod", None), P("prod"), P("prod"), P("prod"),
        P("date", None, None), P("prod"), P("prod"),
    )
    return jax.shard_map(
        on_device, mesh=mesh, in_specs=placed, out_specs=P("date", "prod", None), check_vma=False
    )
```
